512 devices in a mesh: ckpt: 4 (over x), vocab: 128 (over z, y, core).
Axes of the slice: x: 4, y: 8, z: 8, core: 2. Of those that a mesh axis runs over, the one named last changes fastest.
Arguments:
- token_ids: int32 [16384], P('vocab'), may hold values from 0 to 16383, as said below
- grad_values: bfloat16 [4, 16384, 8192], P('ckpt', 'vocab'), may hold values from -6 to 6
- grad_scales: float32 [4, 64, 16384], P('ckpt', None, 'vocab'), may hold values from 0.3 to 3
- tables: bfloat16 [4, 16384, 8192], P('ckpt', 'vocab'), may hold values from -6 to 6
Outputs:
- merged: bfloat16 [16384, 8192], P('vocab', 'ckpt')
The draws below stay inside these ranges and needn't reach their ends.
Inputs may be any that keep to these rules, and one draw needn't show every extreme that they name: The owner of a token is token_ids // 128. Among the 128 tokens of each index of vocab, exactly 64 owners appear, each with exactly 2 tokens; one owner appears in every index's tokens. Ids repeat and some owners are far more frequent than others.
All inputs are finite; a program needn't handle non-finite values.
Results may differ from the reference program's by a relative error of at most 0.018.
Values may be sent and summed in bfloat16 or wider, within the bound.
No kernel may reach another device: no remote copies, remote signals or barrier semaphores. Data moves between devices by JAX's collectives and lax.ppermute only.
A program may use at most 64 MiB of HBM per device.

```python
import math
import jax
import jax.numpy as jnp
from jax import lax

D = 8192
BLK = 128
R_DEV = 128
TOK_DEV = 128
CKPT = 4
CAP = 2
VOCAB = 16384
TOKENS = 16384


def draw_token_ids(key, part):
    owners_all = VOCAB // R_DEV
    chosen = TOK_DEV // CAP
    hotness = jax.random.randint(jax.random.fold_in(key, 1), (owners_all,), 1, 9)
    starred = jax.random.randint(jax.random.fold_in(key, 2), (), 0, owners_all)
    keys = jax.random.split(jax.random.fold_in(key, 3), owners_all)
    positions = jnp.arange(owners_all, dtype=jnp.int32)

    def one_device(dkey):
        noise = jax.random.randint(jax.random.fold_in(dkey, 1), (owners_all,), 0, 4096)
        score = noise * hotness * owners_all + positions
        score = jnp.where(positions == starred, 2 ** 28, score)
        picked = lax.top_k(score, chosen)[1].astype(jnp.int32)
        repeated = jnp.repeat(picked, CAP)
        first = jax.random.randint(jax.random.fold_in(dkey, 2), (TOK_DEV,), 0, R_DEV)
        second = jax.random.randint(jax.random.fold_in(dkey, 3), (TOK_DEV,), 0, R_DEV)
        rows = jnp.minimum(first, second)
        ids = repeated * R_DEV + rows
        order = jax.random.permutation(jax.random.fold_in(dkey, 4), TOK_DEV)
        return ids[order].astype(jnp.int32)
    return jax.vmap(one_device)(keys).reshape(TOKENS)


def block_scale(stream_key, shape, cuts, smallest, top_value):
    level, own = 1.0, jax.random.fold_in(stream_key, 6)
    for axis_at, shards_of in cuts:
        heights = jnp.exp(jax.random.uniform(jax.random.fold_in(own, axis_at), (shards_of,), jnp.float32, smallest / len(cuts), top_value / len(cuts)))
        level = level * jnp.repeat(heights, shape[axis_at] // shards_of).reshape([-1 if axis == axis_at else 1 for axis in range(len(shape))])
    return level


def centred(key, dims, spread, limit, pieces=(), kind=jnp.bfloat16):
    factor_of = block_scale(key, dims, pieces, -0.22, 0.18) if pieces else 1.0
    drawn = jax.random.normal(key, dims, jnp.float32) * spread * factor_of
    return jnp.minimum(jnp.maximum(drawn, -limit), limit).astype(kind)


def setup_inputs(seed: int = 0) -> dict:
    seeds = jax.random.split(jax.random.key(seed), 5)
    token_ids = draw_token_ids(jax.random.fold_in(seeds[4], 71), 0)
    grad_values = centred(seeds[1], (CKPT, TOKENS, D), 1.0, 6.0, ((0, 4), (1, 128)))
    grad_scales = jnp.clip(jnp.exp(math.log(3.0) - 2.3025851 * jax.random.uniform(seeds[2], (CKPT, D // BLK, TOKENS), jnp.float32) ** block_scale(seeds[2], (CKPT, D // BLK, TOKENS), ((0, 4), (2, 128)), -0.2, 0.2)), 0.3, 3.0)
    tables = centred(seeds[3], (CKPT, VOCAB, D), 1.0, 6.0, ((0, 4), (1, 128)))
    return dict(token_ids=token_ids, grad_values=grad_values, grad_scales=grad_scales, tables=tables)


prior_weight = 1.0


def reference(token_ids, grad_values, grad_scales, tables):
    numer = jnp.zeros((VOCAB, D), jnp.float32)
    denom = jnp.zeros((VOCAB, D), jnp.float32)
    for index in range(CKPT):
        scales = grad_scales[index].T
        grads = grad_values[index].astype(jnp.float32).reshape(TOKENS, D // BLK, BLK) * scales[:, :, None]
        squares = (grads * grads).reshape(TOKENS, D).astype(jnp.bfloat16)
        fisher = jax.ops.segment_sum(squares.astype(jnp.float32), token_ids, num_segments=VOCAB)
        weight = (fisher + prior_weight).astype(jnp.bfloat16)
        term = (weight.astype(jnp.float32) * tables[index].astype(jnp.float32)).astype(jnp.bfloat16)
        numer = numer + term.astype(jnp.float32)
        denom = denom + weight.astype(jnp.float32)
    return (numer / denom).astype(jnp.bfloat16)
```

```python
import functools

import jax
import jax.numpy as jnp
from jax import lax
from jax.experimental import pallas as pl
from jax.experimental.pallas import tpu as pltpu
from jax.sharding import PartitionSpec as P

BLK = 128
CAP = 2
SUB = 4

prior_weight = 1.0


def place_kernel(slot_ref, scales_ref, grads_ref, out_ref, match_ref):
    count = grads_ref.shape[0]
    quarter = grads_ref.shape[1]
    rows = out_ref.shape[0]
    cols = quarter // SUB

    @pl.when(pl.program_id(0) == 0)
    def _():
        slot = slot_ref[...]
        for b in range(SUB):
            target = (slot // CAP) * (CAP * SUB) + (slot % CAP) * SUB + b
            hit = lax.broadcasted_iota(jnp.int32, (rows, count), 0) == target
            match_ref[:, b * count : (b + 1) * count] = jnp.where(hit, 1.0, 0.0).astype(jnp.bfloat16)

    scales = scales_ref[...]
    blocks = scales.shape[0]
    scales = jnp.concatenate([scales, jnp.zeros((count - blocks, count), jnp.float32)], axis=0).T
    per = cols // BLK
    stacked = []
    for b in range(SUB):
        pieces = []
        for j in range(b * per, (b + 1) * per):
            grads = grads_ref[:, j * BLK : (j + 1) * BLK].astype(jnp.float32) * scales[:, j : j + 1]
            pieces.append((grads * grads).astype(jnp.bfloat16))
        stacked.append(jnp.concatenate(pieces, axis=1))
    squares = jnp.concatenate(stacked, axis=0)
    out_ref[...] = jnp.dot(
        match_ref[...], squares, preferred_element_type=jnp.float32
    ).astype(jnp.bfloat16)


def select_kernel(target_ref, out_ref):
    hit = lax.broadcasted_iota(jnp.int32, out_ref.shape, 0) == target_ref[...]
    out_ref[...] = jnp.where(hit, 1.0, 0.0).astype(jnp.bfloat16)


def merge_kernel(me_ref, select_ref, arrived_ref, tables_ref, out_ref, numer_ref, denom_ref):
    step = pl.program_id(0)
    rows = out_ref.shape[0]
    cols = arrived_ref.shape[1]

    @pl.when(step == 0)
    def _():
        numer_ref[...] = jnp.zeros_like(numer_ref)
        denom_ref[...] = jnp.zeros_like(denom_ref)

    fisher = jnp.dot(select_ref[...], arrived_ref[...], preferred_element_type=jnp.float32)
    for b in range(SUB):
        at = slice(b * cols, (b + 1) * cols)
        weight = (fisher[b * rows : (b + 1) * rows] + prior_weight).astype(jnp.bfloat16)
        weight = weight.astype(jnp.float32)
        term = (weight * tables_ref[0, :, at].astype(jnp.float32)).astype(jnp.bfloat16)
        numer_ref[:, at] += term.astype(jnp.float32)
        denom_ref[:, at] += weight

    @pl.when(step == pl.num_programs(0) - 1)
    def _():
        out_ref[...] = (numer_ref[...] / denom_ref[...]).astype(jnp.bfloat16)


def per_device(token_ids, grad_values, grad_scales, tables):
    groups = lax.axis_size("vocab")
    ckpts = lax.axis_size("ckpt")
    me = lax.axis_index("ckpt")
    rows = tables.shape[1]
    width = tables.shape[2]
    count = token_ids.shape[0]
    quarter = width // ckpts
    cols = quarter // SUB

    owner = token_ids // rows
    same = owner[:, None] == owner[None, :]
    before = lax.broadcasted_iota(jnp.int32, (count, count), 0) < lax.broadcasted_iota(
        jnp.int32, (count, count), 1
    )
    rank = jnp.sum((same & before).astype(jnp.int32), axis=0)
    slot = owner * CAP + rank
    match = lax.broadcasted_iota(jnp.int32, (groups * CAP, count), 0) == slot[None, :]
    row_tags = (
        jnp.sum(jnp.where(match, (token_ids % rows)[None, :], 0), axis=1)
        .astype(jnp.bfloat16)
        .reshape(groups, CAP)
    )
    arrived_rows = lax.all_to_all(row_tags, "vocab", split_axis=0, concat_axis=0, tiled=True)

    chunk = CAP * SUB
    buffer = pl.pallas_call(
        place_kernel,
        grid=(ckpts,),
        in_specs=[
            pl.BlockSpec((1, count), lambda i: (0, 0)),
            pl.BlockSpec((quarter // BLK, count), lambda i: (i, 0)),
            pl.BlockSpec((count, quarter), lambda i: (0, i)),
        ],
        out_specs=pl.BlockSpec((groups * chunk, cols), lambda i: (i, 0)),
        out_shape=jax.ShapeDtypeStruct((ckpts * groups * chunk, cols), jnp.bfloat16),
        scratch_shapes=[pltpu.VMEM((groups * chunk, SUB * count), jnp.bfloat16)],
        compiler_params=pltpu.CompilerParams(vmem_limit_bytes=56 << 20),
        name="place",
    )(slot[None, :], grad_scales[0], grad_values[0])

    arrived = lax.all_to_all(
        buffer.reshape(ckpts * groups, chunk, cols),
        ("ckpt", "vocab"),
        split_axis=0,
        concat_axis=0,
        tiled=True,
    ).reshape(ckpts * groups * chunk, cols)

    def part(k):
        at = lax.rem(me + k, ckpts) * quarter
        return lax.dynamic_slice(tables[0], (0, at), (rows, quarter))

    held = [part(0)]
    for k in range(1, ckpts):
        held.append(lax.ppermute(part(k), "ckpt", [(i, (i + k) % ckpts) for i in range(ckpts)]))
    held = jnp.stack(held)

    target = arrived_rows.astype(jnp.int32).reshape(groups * CAP, 1) + rows * jnp.arange(
        SUB, dtype=jnp.int32
    )
    select = pl.pallas_call(
        select_kernel,
        out_shape=jax.ShapeDtypeStruct((SUB * rows, groups * chunk), jnp.bfloat16),
        compiler_params=pltpu.CompilerParams(vmem_limit_bytes=16 << 20),
        name="select",
    )(target.reshape(1, groups * chunk))

    return pl.pallas_call(
        merge_kernel,
        grid_spec=pltpu.PrefetchScalarGridSpec(
            num_scalar_prefetch=1,
            grid=(ckpts,),
            in_specs=[
                pl.BlockSpec((SUB * rows, groups * chunk), lambda k, me: (0, 0)),
                pl.BlockSpec(
                    (groups * chunk, cols), lambda k, me: (lax.rem(me[0] - k + ckpts, ckpts), 0)
                ),
                pl.BlockSpec((1, rows, quarter), lambda k, me: (k, 0, 0)),
            ],
            out_specs=pl.BlockSpec((rows, quarter), lambda k, me: (0, 0)),
            scratch_shapes=[
                pltpu.VMEM((rows, quarter), jnp.float32),
                pltpu.VMEM((rows, quarter), jnp.float32),
            ],
        ),
        out_shape=jax.ShapeDtypeStruct((rows, quarter), jnp.bfloat16),
        compiler_params=pltpu.CompilerParams(vmem_limit_bytes=32 << 20),
        name="merge",
    )(me.astype(jnp.int32)[None], select, arrived, held)


def solution(mesh):
    return jax.shard_map(
        per_device,
        mesh=mesh,
        in_specs=(
            P("vocab"),
            P("ckpt", "vocab", None),
            P("ckpt", None, "vocab"),
            P("ckpt", "vocab", None),
        ),
        out_specs=P("vocab", "ckpt"),
        check_vma=False,
    )
```

```python
import functools

import jax
import jax.numpy as jnp
from jax import lax
from jax.experimental import pallas as pl
from jax.experimental.pallas import tpu as pltpu
from jax.sharding import PartitionSpec as P

BLK = 128
CAP = 2
SUB = 4
NEAR = 32

prior_weight = 1.0


def place_kernel(slot_ref, scales_ref, grads_hbm, out_hbm, grads, placed, match, squares, in_sems, out_sems):
    parts, count, quarter = grads.shape
    rows = match.shape[0]
    cols = quarter // SUB
    copies_in = []
    for i in range(parts):
        copy = pltpu.make_async_copy(
            grads_hbm.at[:, i * quarter : (i + 1) * quarter], grads.at[i], in_sems.at[i]
        )
        copy.start()
        copies_in.append(copy)
    slot = slot_ref[...]
    for b in range(SUB):
        target = (slot // CAP) * (CAP * SUB) + (slot % CAP) * SUB + b
        hit = lax.broadcasted_iota(jnp.int32, (rows, count), 0) == target
        match[:, b * count : (b + 1) * count] = jnp.where(hit, 1.0, 0.0).astype(jnp.bfloat16)
    scales = scales_ref[...]
    blocks = scales.shape[0]
    scales = jnp.concatenate([scales, jnp.zeros((-blocks % BLK, count), jnp.float32)], axis=0).T
    per = cols // BLK
    copies_out = []
    for i in range(parts):
        copies_in[i].wait()
        for j in range(SUB * per):
            at = i * SUB * per + j
            scaled = grads[i, :, j * BLK : (j + 1) * BLK].astype(jnp.float32) * scales[:, at : at + 1]
            b, n = divmod(j, per)
            squares[i, b * count : (b + 1) * count, n * BLK : (n + 1) * BLK] = (
                scaled * scaled
            ).astype(jnp.bfloat16)
        here = slice(i * rows, (i + 1) * rows)
        placed[here, :] = jnp.dot(
            match[...], squares[i], preferred_element_type=jnp.float32
        ).astype(jnp.bfloat16)
        copy = pltpu.make_async_copy(placed.at[here], out_hbm.at[here], out_sems.at[i])
        copy.start()
        copies_out.append(copy)
    for copy in copies_out:
        copy.wait()


def select_kernel(target_ref, out_ref):
    hit = lax.broadcasted_iota(jnp.int32, out_ref.shape, 0) == target_ref[...]
    out_ref[...] = jnp.where(hit, 1.0, 0.0).astype(jnp.bfloat16)


def merge_kernel(me_ref, select_ref, arrived_hbm, tables_ref, out_ref, arrived, fisher, sems):
    parts, depth, cols = arrived.shape
    rows = out_ref.shape[0]
    copies = []
    for k in range(parts):
        at = pl.multiple_of(lax.rem(me_ref[0] + (parts - k), parts) * depth, depth)
        copy = pltpu.make_async_copy(arrived_hbm.at[pl.ds(at, depth)], arrived.at[k], sems.at[k])
        copy.start()
        copies.append(copy)
    for k in range(parts):
        copies[k].wait()
        fisher[k] = jnp.dot(select_ref[...], arrived[k], preferred_element_type=jnp.float32)
    for b in range(SUB):
        at = slice(b * cols, (b + 1) * cols)
        numer = denom = None
        for k in range(parts):
            weight = (fisher[k, b * rows : (b + 1) * rows] + prior_weight).astype(jnp.bfloat16)
            weight = weight.astype(jnp.float32)
            term = (weight * tables_ref[k, :, at].astype(jnp.float32)).astype(jnp.bfloat16)
            term = term.astype(jnp.float32)
            numer = term if numer is None else numer + term
            denom = weight if denom is None else denom + weight
        out_ref[:, at] = (numer / denom).astype(jnp.bfloat16)


def per_device(token_ids, grad_values, grad_scales, tables):
    groups = lax.axis_size("vocab")
    ckpts = lax.axis_size("ckpt")
    me = lax.axis_index("ckpt")
    rows = tables.shape[1]
    width = tables.shape[2]
    count = token_ids.shape[0]
    quarter = width // ckpts
    cols = quarter // SUB

    near = min(NEAR, groups)
    far = groups // near
    owner = lax.div(token_ids, rows)
    same = owner[:, None] == owner[None, :]
    before = lax.broadcasted_iota(jnp.int32, (count, count), 0) < lax.broadcasted_iota(
        jnp.int32, (count, count), 1
    )
    rank = jnp.sum((same & before).astype(jnp.int32), axis=0)
    slot = owner * CAP + rank
    tag_slot = (lax.rem(owner, near) * far + lax.div(owner, near)) * CAP + rank
    match = lax.broadcasted_iota(jnp.int32, (groups * CAP, count), 0) == tag_slot[None, :]
    row_tags = jnp.sum(jnp.where(match, lax.rem(token_ids, rows)[None, :], 0), axis=1)
    near_rows = lax.all_to_all(
        row_tags.reshape(near, far * CAP),
        "vocab",
        split_axis=0,
        concat_axis=0,
        axis_index_groups=[[f * near + n for n in range(near)] for f in range(far)],
        tiled=True,
    )

    chunk = CAP * SUB
    buffer = pl.pallas_call(
        place_kernel,
        in_specs=[
            pl.BlockSpec(memory_space=pltpu.VMEM),
            pl.BlockSpec(memory_space=pltpu.VMEM),
            pl.BlockSpec(memory_space=pltpu.HBM),
        ],
        out_specs=pl.BlockSpec(memory_space=pltpu.HBM),
        out_shape=jax.ShapeDtypeStruct((ckpts * groups * chunk, cols), jnp.bfloat16),
        scratch_shapes=[
            pltpu.VMEM((ckpts, count, quarter), jnp.bfloat16),
            pltpu.VMEM((ckpts * groups * chunk, cols), jnp.bfloat16),
            pltpu.VMEM((groups * chunk, SUB * count), jnp.bfloat16),
            pltpu.VMEM((ckpts, SUB * count, cols), jnp.bfloat16),
            pltpu.SemaphoreType.DMA((ckpts,)),
            pltpu.SemaphoreType.DMA((ckpts,)),
        ],
        compiler_params=pltpu.CompilerParams(vmem_limit_bytes=56 << 20),
        name="place",
    )(slot[None, :], grad_scales[0], grad_values[0])

    arrived = lax.all_to_all(
        buffer.reshape(ckpts * groups, chunk, cols),
        ("ckpt", "vocab"),
        split_axis=0,
        concat_axis=0,
        tiled=True,
    ).reshape(ckpts * groups * chunk, cols)

    def part(k):
        at = lax.rem(me + k, ckpts) * quarter
        return lax.dynamic_slice(tables[0], (0, at), (rows, quarter))

    held = [part(0)]
    for k in (1, 2, 3):
        piece = part(k)
        if k == 3:
            piece, held[1] = lax.optimization_barrier((piece, held[1]))
        held.append(lax.ppermute(piece, "ckpt", [(i, (i + k) % ckpts) for i in range(ckpts)]))
    held = jnp.stack(held)

    far_me = lax.div(lax.axis_index("vocab"), near)
    near_rows = near_rows.reshape(near, far, CAP)
    passed = []
    for m in range(far):
        piece = lax.dynamic_slice(
            near_rows, (0, lax.rem(far_me + (far - m), far), 0), (near, 1, CAP)
        ).reshape(1, near * CAP)
        if m:
            piece = lax.ppermute(
                piece, "vocab", [(v, (v + groups - m * near) % groups) for v in range(groups)]
            )
        passed.append(piece)
    passed = jnp.concatenate(passed + passed, axis=0)
    arrived_rows = lax.dynamic_slice(
        passed, (lax.rem(far - far_me, far), 0), (far, near * CAP)
    ).reshape(groups * CAP, 1)
    target = arrived_rows + rows * jnp.arange(SUB, dtype=jnp.int32)
    select = pl.pallas_call(
        select_kernel,
        out_shape=jax.ShapeDtypeStruct((SUB * rows, groups * chunk), jnp.bfloat16),
        compiler_params=pltpu.CompilerParams(vmem_limit_bytes=16 << 20),
        name="select",
    )(target.reshape(1, groups * chunk))

    return pl.pallas_call(
        merge_kernel,
        in_specs=[
            pl.BlockSpec(memory_space=pltpu.SMEM),
            pl.BlockSpec(memory_space=pltpu.VMEM),
            pl.BlockSpec(memory_space=pltpu.HBM),
            pl.BlockSpec(memory_space=pltpu.VMEM),
        ],
        out_specs=pl.BlockSpec(memory_space=pltpu.VMEM),
        out_shape=jax.ShapeDtypeStruct((rows, quarter), jnp.bfloat16),
        scratch_shapes=[
            pltpu.VMEM((ckpts, groups * chunk, cols), jnp.bfloat16),
            pltpu.VMEM((ckpts, SUB * rows, cols), jnp.float32),
            pltpu.SemaphoreType.DMA((ckpts,)),
        ],
        compiler_params=pltpu.CompilerParams(vmem_limit_bytes=32 << 20),
        name="merge",
    )(me.astype(jnp.int32)[None], select, arrived, held)


def solution(mesh):
    return jax.shard_map(
        per_device,
        mesh=mesh,
        in_specs=(
            P("vocab"),
            P("ckpt", "vocab", None),
            P("ckpt", None, "vocab"),
            P("ckpt", "vocab", None),
        ),
        out_specs=P("vocab", "ckpt"),
        check_vma=False,
    )
```

```python
import functools

import jax
import jax.numpy as jnp
from jax import lax
from jax.experimental import pallas as pl
from jax.experimental.pallas import tpu as pltpu
from jax.sharding import PartitionSpec as P

BLK = 128
CAP = 2
SUB = 4
CORES = 2

prior_weight = 1.0


def place_kernel(slot_ref, scales_ref, grads_hbm, out_hbm, grads, placed, match, squares, in_sems, out_sems):
    parts, count, quarter = grads.shape
    rows = match.shape[0]
    cols = quarter // SUB
    copies_in = []
    for i in range(parts):
        copy = pltpu.make_async_copy(
            grads_hbm.at[:, i * quarter : (i + 1) * quarter], grads.at[i], in_sems.at[i]
        )
        copy.start()
        copies_in.append(copy)
    slot = slot_ref[...]
    for b in range(SUB):
        target = (slot // CAP) * (CAP * SUB) + (slot % CAP) * SUB + b
        hit = lax.broadcasted_iota(jnp.int32, (rows, count), 0) == target
        match[:, b * count : (b + 1) * count] = jnp.where(hit, 1.0, 0.0).astype(jnp.bfloat16)
    scales = scales_ref[...]
    blocks = scales.shape[0]
    scales = jnp.concatenate([scales, jnp.zeros((-blocks % BLK, count), jnp.float32)], axis=0).T
    per = cols // BLK
    copies_out = []
    for copy in copies_in:
        copy.wait()
    for i in range(parts):
        for j in range(SUB * per):
            at = i * SUB * per + j
            scaled = grads[i, :, j * BLK : (j + 1) * BLK].astype(jnp.float32) * scales[:, at : at + 1]
            b, n = divmod(j, per)
            squares[i, b * count : (b + 1) * count, n * BLK : (n + 1) * BLK] = (
                scaled * scaled
            ).astype(jnp.bfloat16)
        here = slice(i * rows, (i + 1) * rows)
        placed[here, :] = jnp.dot(
            match[...], squares[i], preferred_element_type=jnp.float32
        ).astype(jnp.bfloat16)
        copy = pltpu.make_async_copy(placed.at[here], out_hbm.at[here], out_sems.at[i])
        copy.start()
        copies_out.append(copy)
    for copy in copies_out:
        copy.wait()


def select_kernel(target_ref, out_ref):
    hit = lax.broadcasted_iota(jnp.int32, out_ref.shape, 0) == target_ref[...]
    out_ref[...] = jnp.where(hit, 1.0, 0.0).astype(jnp.bfloat16)


def merge_kernel(me_ref, select_ref, arrived_hbm, tables_ref, out_ref, arrived, numer, denom, sems):
    parts, depth, cols = arrived.shape
    rows = out_ref.shape[0]
    copies = []
    for k in range(parts):
        at = pl.multiple_of(lax.rem(me_ref[0] + (parts - k), parts) * depth, depth)
        copy = pltpu.make_async_copy(arrived_hbm.at[pl.ds(at, depth)], arrived.at[k], sems.at[k])
        copy.start()
        copies.append(copy)
    for k in range(parts):
        copies[k].wait()
        fisher = jnp.dot(select_ref[...], arrived[k], preferred_element_type=jnp.float32)
        for b in range(SUB):
            at = slice(b * cols, (b + 1) * cols)
            weight = (fisher[b * rows : (b + 1) * rows] + prior_weight).astype(jnp.bfloat16)
            weight = weight.astype(jnp.float32)
            term = (weight * tables_ref[k, :, at].astype(jnp.float32)).astype(jnp.bfloat16)
            term = term.astype(jnp.float32)
            if k == 0:
                numer[:, at] = term
                denom[:, at] = weight
            elif k < parts - 1:
                numer[:, at] += term
                denom[:, at] += weight
            else:
                out_ref[:, at] = ((numer[:, at] + term) / (denom[:, at] + weight)).astype(jnp.bfloat16)


def per_device(token_ids, grad_values, grad_scales, tables):
    groups = lax.axis_size("vocab")
    ckpts = lax.axis_size("ckpt")
    me = lax.axis_index("ckpt")
    rows = tables.shape[1]
    width = tables.shape[2]
    count = token_ids.shape[0]
    quarter = width // ckpts
    cols = quarter // SUB

    chips = groups // CORES
    owner = lax.div(token_ids, rows)
    same = owner[:, None] == owner[None, :]
    before = lax.broadcasted_iota(jnp.int32, (count, count), 0) < lax.broadcasted_iota(
        jnp.int32, (count, count), 1
    )
    rank = jnp.sum((same & before).astype(jnp.int32), axis=0)
    slot = owner * CAP + rank
    match = lax.broadcasted_iota(jnp.int32, (groups * CAP, count), 0) == slot[None, :]
    row_tags = jnp.sum(jnp.where(match, lax.rem(token_ids, rows)[None, :], 0), axis=1)
    chip_rows = lax.all_to_all(
        row_tags.reshape(chips, CORES * CAP),
        "vocab",
        split_axis=0,
        concat_axis=0,
        axis_index_groups=[[n * CORES + core for n in range(chips)] for core in range(CORES)],
        tiled=True,
    )

    chunk = CAP * SUB
    buffer = pl.pallas_call(
        place_kernel,
        in_specs=[
            pl.BlockSpec(memory_space=pltpu.VMEM),
            pl.BlockSpec(memory_space=pltpu.VMEM),
            pl.BlockSpec(memory_space=pltpu.HBM),
        ],
        out_specs=pl.BlockSpec(memory_space=pltpu.HBM),
        out_shape=jax.ShapeDtypeStruct((ckpts * groups * chunk, cols), jnp.bfloat16),
        scratch_shapes=[
            pltpu.VMEM((ckpts, count, quarter), jnp.bfloat16),
            pltpu.VMEM((ckpts * groups * chunk, cols), jnp.bfloat16),
            pltpu.VMEM((groups * chunk, SUB * count), jnp.bfloat16),
            pltpu.VMEM((ckpts, SUB * count, cols), jnp.bfloat16),
            pltpu.SemaphoreType.DMA((ckpts,)),
            pltpu.SemaphoreType.DMA((ckpts,)),
        ],
        compiler_params=pltpu.CompilerParams(vmem_limit_bytes=56 << 20),
        name="place",
    )(slot[None, :], grad_scales[0], grad_values[0])

    arrived = lax.all_to_all(
        buffer.reshape(ckpts * groups, chunk, cols),
        ("ckpt", "vocab"),
        split_axis=0,
        concat_axis=0,
        tiled=True,
    ).reshape(ckpts * groups * chunk, cols)

    def part(k):
        at = lax.rem(me + k, ckpts) * quarter
        return lax.dynamic_slice(tables[0], (0, at), (rows, quarter))

    held = [part(0)]
    for k in range(1, ckpts):
        held.append(lax.ppermute(part(k), "ckpt", [(i, (i + k) % ckpts) for i in range(ckpts)]))
    held = jnp.stack(held)

    core = lax.rem(lax.axis_index("vocab"), CORES)
    chip_rows = chip_rows.reshape(chips, CORES, CAP).transpose(1, 2, 0)
    mine = lax.dynamic_slice(chip_rows, (core, 0, 0), (1, CAP, chips))[0]
    other = lax.dynamic_slice(chip_rows, (CORES - 1 - core, 0, 0), (1, CAP, chips))[0]
    other = lax.ppermute(other, "vocab", [(v, v ^ 1) for v in range(groups)])
    even, odd = jnp.where(core == 0, mine, other), jnp.where(core == 0, other, mine)
    arrived_rows = jnp.stack([even, odd]).transpose(2, 0, 1).reshape(groups * CAP, 1)
    target = arrived_rows + rows * jnp.arange(SUB, dtype=jnp.int32)
    select = pl.pallas_call(
        select_kernel,
        out_shape=jax.ShapeDtypeStruct((SUB * rows, groups * chunk), jnp.bfloat16),
        compiler_params=pltpu.CompilerParams(vmem_limit_bytes=16 << 20),
        name="select",
    )(target.reshape(1, groups * chunk))

    return pl.pallas_call(
        merge_kernel,
        in_specs=[
            pl.BlockSpec(memory_space=pltpu.SMEM),
            pl.BlockSpec(memory_space=pltpu.VMEM),
            pl.BlockSpec(memory_space=pltpu.HBM),
            pl.BlockSpec(memory_space=pltpu.VMEM),
        ],
        out_specs=pl.BlockSpec(memory_space=pltpu.VMEM),
        out_shape=jax.ShapeDtypeStruct((rows, quarter), jnp.bfloat16),
        scratch_shapes=[
            pltpu.VMEM((ckpts, groups * chunk, cols), jnp.bfloat16),
            pltpu.VMEM((rows, quarter), jnp.float32),
            pltpu.VMEM((rows, quarter), jnp.float32),
            pltpu.SemaphoreType.DMA((ckpts,)),
        ],
        compiler_params=pltpu.CompilerParams(vmem_limit_bytes=32 << 20),
        name="merge",
    )(me.astype(jnp.int32)[None], select, arrived, held)


def solution(mesh):
    return jax.shard_map(
        per_device,
        mesh=mesh,
        in_specs=(
            P("vocab"),
            P("ckpt", "vocab", None),
            P("ckpt", None, "vocab"),
            P("ckpt", "vocab", None),
        ),
        out_specs=P("vocab", "ckpt"),
        check_vma=False,
    )
```

```python
import functools

import jax
import jax.numpy as jnp
from jax import lax
from jax.experimental import pallas as pl
from jax.experimental.pallas import tpu as pltpu
from jax.sharding import PartitionSpec as P

BLK = 128
CAP = 2
SUB = 4
NEAR = 32

prior_weight = 1.0


def place_kernel(slot_hbm, scales_hbm, grads_hbm, out_hbm, slot_ref, scales_ref, grads, placed, match, squares, sems, out_sems):
    parts, count, quarter = grads.shape
    rows = match.shape[0]
    cols = quarter // SUB
    copies_in = [
        pltpu.make_async_copy(slot_hbm, slot_ref, sems.at[parts]),
        pltpu.make_async_copy(scales_hbm, scales_ref, sems.at[parts + 1]),
    ]
    for i in range(parts):
        copies_in.append(
            pltpu.make_async_copy(grads_hbm.at[:, i * quarter : (i + 1) * quarter], grads.at[i], sems.at[i])
        )
    for copy in copies_in:
        copy.start()
    copies_in[0].wait()
    slot = slot_ref[...]
    for b in range(SUB):
        target = (slot // CAP) * (CAP * SUB) + (slot % CAP) * SUB + b
        hit = lax.broadcasted_iota(jnp.int32, (rows, count), 0) == target
        match[:, b * count : (b + 1) * count] = jnp.where(hit, 1.0, 0.0).astype(jnp.bfloat16)
    for copy in copies_in[1:]:
        copy.wait()
    scales = scales_ref[...]
    blocks = scales.shape[0]
    scales = jnp.concatenate([scales, jnp.zeros((-blocks % BLK, count), jnp.float32)], axis=0).T
    per = cols // BLK
    copies_out = []
    for i in range(parts):
        for j in range(SUB * per):
            at = i * SUB * per + j
            scaled = grads[i, :, j * BLK : (j + 1) * BLK].astype(jnp.float32) * scales[:, at : at + 1]
            b, n = divmod(j, per)
            squares[i, b * count : (b + 1) * count, n * BLK : (n + 1) * BLK] = (
                scaled * scaled
            ).astype(jnp.bfloat16)
        here = slice(i * rows, (i + 1) * rows)
        placed[here, :] = jnp.dot(
            match[...], squares[i], preferred_element_type=jnp.float32
        ).astype(jnp.bfloat16)
        copy = pltpu.make_async_copy(placed.at[here], out_hbm.at[here], out_sems.at[i])
        copy.start()
        copies_out.append(copy)
    for copy in copies_out:
        copy.wait()


def merge_kernel(me_ref, target_ref, arrived_hbm, tables_hbm, out_hbm, arrived, tables, select, numer, denom, out, sems, table_sems, out_sems):
    parts, depth, cols = arrived.shape
    rows = out.shape[0]
    copies = []
    for k in range(parts):
        at = pl.multiple_of(lax.rem(me_ref[0] + (parts - k), parts) * depth, depth)
        copies.append(
            (
                pltpu.make_async_copy(arrived_hbm.at[pl.ds(at, depth)], arrived.at[k], sems.at[k]),
                pltpu.make_async_copy(tables_hbm.at[k], tables.at[k], table_sems.at[k]),
            )
        )
        for copy in copies[k]:
            copy.start()
    hit = lax.broadcasted_iota(jnp.int32, select.shape, 0) == target_ref[...]
    select[...] = jnp.where(hit, 1.0, 0.0).astype(jnp.bfloat16)
    copies_out = []
    for k in range(parts):
        for copy in copies[k]:
            copy.wait()
        fisher = jnp.dot(select[...], arrived[k], preferred_element_type=jnp.float32)
        for b in range(SUB):
            at = slice(b * cols, (b + 1) * cols)
            weight = (fisher[b * rows : (b + 1) * rows] + prior_weight).astype(jnp.bfloat16)
            weight = weight.astype(jnp.float32)
            term = (weight * tables[k, :, at].astype(jnp.float32)).astype(jnp.bfloat16)
            term = term.astype(jnp.float32)
            if k == 0:
                numer[:, at] = term
                denom[:, at] = weight
            elif k < parts - 1:
                numer[:, at] += term
                denom[:, at] += weight
            else:
                out[:, at] = ((numer[:, at] + term) / (denom[:, at] + weight)).astype(jnp.bfloat16)
                copy = pltpu.make_async_copy(out.at[:, at], out_hbm.at[:, at], out_sems.at[b])
                copy.start()
                copies_out.append(copy)
    for copy in copies_out:
        copy.wait()


def per_device(token_ids, grad_values, grad_scales, tables):
    groups = lax.axis_size("vocab")
    ckpts = lax.axis_size("ckpt")
    me = lax.axis_index("ckpt")
    rows = tables.shape[1]
    width = tables.shape[2]
    count = token_ids.shape[0]
    quarter = width // ckpts
    cols = quarter // SUB

    near = min(NEAR, groups)
    far = groups // near
    owner = lax.div(token_ids, rows)
    same = owner[:, None] == owner[None, :]
    before = lax.broadcasted_iota(jnp.int32, (count, count), 0) < lax.broadcasted_iota(
        jnp.int32, (count, count), 1
    )
    rank = jnp.sum((same & before).astype(jnp.int32), axis=0)
    slot = owner * CAP + rank
    at = lax.broadcasted_iota(jnp.uint32, (groups * CAP, count), 0)
    spot = at // CAP
    spot = ((spot % far) * near + spot // far) * CAP + at % CAP
    match = spot.astype(jnp.int32) == slot[None, :]
    row_tags = jnp.sum(jnp.where(match, lax.rem(token_ids, rows)[None, :], 0), axis=1)
    near_rows = lax.all_to_all(
        row_tags.reshape(near, far * CAP),
        "vocab",
        split_axis=0,
        concat_axis=0,
        axis_index_groups=[[f * near + n for n in range(near)] for f in range(far)],
        tiled=True,
    )

    chunk = CAP * SUB
    buffer = pl.pallas_call(
        place_kernel,
        in_specs=[
            pl.BlockSpec(memory_space=pl.ANY),
            pl.BlockSpec(memory_space=pl.ANY),
            pl.BlockSpec(memory_space=pl.ANY),
        ],
        out_specs=pl.BlockSpec(memory_space=pltpu.HBM),
        out_shape=jax.ShapeDtypeStruct((ckpts * groups * chunk, cols), jnp.bfloat16),
        scratch_shapes=[
            pltpu.VMEM((1, count), jnp.int32),
            pltpu.VMEM((width // BLK, count), jnp.float32),
            pltpu.VMEM((ckpts, count, quarter), jnp.bfloat16),
            pltpu.VMEM((ckpts * groups * chunk, cols), jnp.bfloat16),
            pltpu.VMEM((groups * chunk, SUB * count), jnp.bfloat16),
            pltpu.VMEM((ckpts, SUB * count, cols), jnp.bfloat16),
            pltpu.SemaphoreType.DMA((ckpts + 2,)),
            pltpu.SemaphoreType.DMA((ckpts,)),
        ],
        compiler_params=pltpu.CompilerParams(vmem_limit_bytes=56 << 20),
        name="place",
    )(slot[None, :], grad_scales[0], grad_values[0])

    arrived = lax.all_to_all(
        buffer.reshape(ckpts * groups, chunk, cols),
        ("ckpt", "vocab"),
        split_axis=0,
        concat_axis=0,
        tiled=True,
    ).reshape(ckpts * groups * chunk, cols)

    def part(k):
        at = lax.rem(me + k, ckpts) * quarter
        return lax.dynamic_slice(tables[0], (0, at), (rows, quarter))

    held = [part(0)]
    for k in (1, 2, 3):
        piece = part(k)
        if k == 3:
            piece, held[1] = lax.optimization_barrier((piece, held[1]))
        held.append(lax.ppermute(piece, "ckpt", [(i, (i + k) % ckpts) for i in range(ckpts)]))
    held = jnp.stack(held)

    far_me = lax.div(lax.axis_index("vocab"), near)
    near_rows = near_rows.reshape(near, far, CAP)
    passed = []
    for m in range(far):
        piece = lax.dynamic_slice(
            near_rows, (0, lax.rem(far_me + (far - m), far), 0), (near, 1, CAP)
        ).reshape(1, near * CAP)
        if m:
            piece = lax.ppermute(
                piece, "vocab", [(v, (v + groups - m * near) % groups) for v in range(groups)]
            )
        passed.append(piece)
    passed = jnp.concatenate(passed + passed, axis=0)
    arrived_rows = lax.dynamic_slice(
        passed, (lax.rem(far - far_me, far), 0), (far, near * CAP)
    ).reshape(groups * CAP, 1)
    target = arrived_rows + rows * jnp.arange(SUB, dtype=jnp.int32)
    return pl.pallas_call(
        merge_kernel,
        in_specs=[
            pl.BlockSpec(memory_space=pltpu.SMEM),
            pl.BlockSpec(memory_space=pltpu.VMEM),
            pl.BlockSpec(memory_space=pl.ANY),
            pl.BlockSpec(memory_space=pl.ANY),
        ],
        out_specs=pl.BlockSpec(memory_space=pltpu.HBM),
        out_shape=jax.ShapeDtypeStruct((rows, quarter), jnp.bfloat16),
        scratch_shapes=[
            pltpu.VMEM((ckpts, groups * chunk, cols), jnp.bfloat16),
            pltpu.VMEM((ckpts, rows, quarter), jnp.bfloat16),
            pltpu.VMEM((SUB * rows, groups * chunk), jnp.bfloat16),
            pltpu.VMEM((rows, quarter), jnp.float32),
            pltpu.VMEM((rows, quarter), jnp.float32),
            pltpu.VMEM((rows, quarter), jnp.bfloat16),
            pltpu.SemaphoreType.DMA((ckpts,)),
            pltpu.SemaphoreType.DMA((ckpts,)),
            pltpu.SemaphoreType.DMA((SUB,)),
        ],
        compiler_params=pltpu.CompilerParams(vmem_limit_bytes=32 << 20),
        name="merge",
    )(me.astype(jnp.int32)[None], target.reshape(1, groups * chunk), arrived, held)


def solution(mesh):
    return jax.shard_map(
        per_device,
        mesh=mesh,
        in_specs=(
            P("vocab"),
            P("ckpt", "vocab", None),
            P("ckpt", None, "vocab"),
            P("ckpt", "vocab", None),
        ),
        out_specs=P("vocab", "ckpt"),
        check_vma=False,
    )
```

```python
import functools

import jax
import jax.numpy as jnp
from jax import lax
from jax.experimental import pallas as pl
from jax.experimental.pallas import tpu as pltpu
from jax.sharding import PartitionSpec as P

BLK = 128
CAP = 2
SUB = 4
NEAR = 32

prior_weight = 1.0


def place_kernel(slot_hbm, scales_hbm, grads_hbm, out_hbm, slot_ref, scales_ref, grads, placed, match, squares, sems, out_sems):
    parts, count, quarter = grads.shape
    rows = match.shape[0]
    cols = quarter // SUB
    copies_in = [
        pltpu.make_async_copy(slot_hbm, slot_ref, sems.at[parts]),
        pltpu.make_async_copy(scales_hbm, scales_ref, sems.at[parts + 1]),
    ]
    for i in range(parts):
        copies_in.append(
            pltpu.make_async_copy(grads_hbm.at[:, i * quarter : (i + 1) * quarter], grads.at[i], sems.at[i])
        )
    for copy in copies_in:
        copy.start()
    copies_in[0].wait()
    slot = slot_ref[...]
    for b in range(SUB):
        target = (slot // CAP) * (CAP * SUB) + (slot % CAP) * SUB + b
        hit = lax.broadcasted_iota(jnp.int32, (rows, count), 0) == target
        match[:, b * count : (b + 1) * count] = jnp.where(hit, 1.0, 0.0).astype(jnp.bfloat16)
    for copy in copies_in[1:]:
        copy.wait()
    scales = scales_ref[...]
    blocks = scales.shape[0]
    scales = jnp.concatenate([scales, jnp.zeros((-blocks % BLK, count), jnp.float32)], axis=0).T
    per = cols // BLK
    copies_out = []
    for i in range(parts):
        for j in range(SUB * per):
            at = i * SUB * per + j
            scaled = grads[i, :, j * BLK : (j + 1) * BLK].astype(jnp.float32) * scales[:, at : at + 1]
            b, n = divmod(j, per)
            squares[i, b * count : (b + 1) * count, n * BLK : (n + 1) * BLK] = (
                scaled * scaled
            ).astype(jnp.bfloat16)
        here = slice(i * rows, (i + 1) * rows)
        placed[here, :] = jnp.dot(
            match[...], squares[i], preferred_element_type=jnp.float32
        ).astype(jnp.bfloat16)
        copy = pltpu.make_async_copy(placed.at[here], out_hbm.at[here], out_sems.at[i])
        copy.start()
        copies_out.append(copy)
    for copy in copies_out:
        copy.wait()


def merge_kernel(target_hbm, arrived_hbm, tables_hbm, out_hbm, target_ref, arrived, tables, select, numer, denom, out, sems, table_sems, out_sems):
    parts, depth, cols = arrived.shape
    rows = out.shape[0]
    me = lax.axis_index("ckpt")
    tags = pltpu.make_async_copy(target_hbm, target_ref, sems.at[parts])
    tags.start()
    copies = []
    for k in range(parts):
        at = pl.multiple_of(lax.rem(me + (parts - k), parts) * depth, depth)
        copies.append(
            (
                pltpu.make_async_copy(arrived_hbm.at[pl.ds(at, depth)], arrived.at[k], sems.at[k]),
                pltpu.make_async_copy(tables_hbm.at[k], tables.at[k], table_sems.at[k]),
            )
        )
        for copy in copies[k]:
            copy.start()
    tags.wait()
    hit = lax.broadcasted_iota(jnp.int32, select.shape, 0) == target_ref[...]
    select[...] = jnp.where(hit, 1.0, 0.0).astype(jnp.bfloat16)
    copies_out = []
    for k in range(parts):
        copies[k][0].wait()
        fisher = jnp.dot(select[...], arrived[k], preferred_element_type=jnp.float32)
        copies[k][1].wait()
        for b in range(SUB):
            at = slice(b * cols, (b + 1) * cols)
            weight = (fisher[b * rows : (b + 1) * rows] + prior_weight).astype(jnp.bfloat16)
            weight = weight.astype(jnp.float32)
            term = (weight * tables[k, :, at].astype(jnp.float32)).astype(jnp.bfloat16)
            term = term.astype(jnp.float32)
            if k == 0:
                numer[:, at] = term
                denom[:, at] = weight
            elif k < parts - 1:
                numer[:, at] += term
                denom[:, at] += weight
            else:
                out[:, at] = ((numer[:, at] + term) / (denom[:, at] + weight)).astype(jnp.bfloat16)
                copy = pltpu.make_async_copy(out.at[:, at], out_hbm.at[:, at], out_sems.at[b])
                copy.start()
                copies_out.append(copy)
    for copy in copies_out:
        copy.wait()


def per_device(token_ids, grad_values, grad_scales, tables):
    groups = lax.axis_size("vocab")
    ckpts = lax.axis_size("ckpt")
    me = lax.axis_index("ckpt")
    rows = tables.shape[1]
    width = tables.shape[2]
    count = token_ids.shape[0]
    quarter = width // ckpts
    cols = quarter // SUB

    near = min(NEAR, groups)
    far = groups // near
    owner = lax.div(token_ids, rows)
    same = owner[:, None] == owner[None, :]
    before = lax.broadcasted_iota(jnp.int32, (count, count), 0) < lax.broadcasted_iota(
        jnp.int32, (count, count), 1
    )
    rank = jnp.sum((same & before).astype(jnp.int32), axis=0)
    slot = owner * CAP + rank
    at = lax.broadcasted_iota(jnp.uint32, (groups * CAP, count), 0)
    spot = at // CAP
    spot = ((spot % far) * near + spot // far) * CAP + at % CAP
    match = spot.astype(jnp.int32) == slot[None, :]
    row_tags = jnp.sum(jnp.where(match, lax.rem(token_ids, rows)[None, :], 0), axis=1)
    near_rows = lax.all_to_all(
        row_tags.reshape(near, far * CAP),
        "vocab",
        split_axis=0,
        concat_axis=0,
        axis_index_groups=[[f * near + n for n in range(near)] for f in range(far)],
        tiled=True,
    )

    chunk = CAP * SUB
    buffer = pl.pallas_call(
        place_kernel,
        in_specs=[
            pl.BlockSpec(memory_space=pl.ANY),
            pl.BlockSpec(memory_space=pl.ANY),
            pl.BlockSpec(memory_space=pl.ANY),
        ],
        out_specs=pl.BlockSpec(memory_space=pltpu.HBM),
        out_shape=jax.ShapeDtypeStruct((ckpts * groups * chunk, cols), jnp.bfloat16),
        scratch_shapes=[
            pltpu.VMEM((1, count), jnp.int32),
            pltpu.VMEM((width // BLK, count), jnp.float32),
            pltpu.VMEM((ckpts, count, quarter), jnp.bfloat16),
            pltpu.VMEM((ckpts * groups * chunk, cols), jnp.bfloat16),
            pltpu.VMEM((groups * chunk, SUB * count), jnp.bfloat16),
            pltpu.VMEM((ckpts, SUB * count, cols), jnp.bfloat16),
            pltpu.SemaphoreType.DMA((ckpts + 2,)),
            pltpu.SemaphoreType.DMA((ckpts,)),
        ],
        compiler_params=pltpu.CompilerParams(vmem_limit_bytes=56 << 20),
        name="place",
    )(slot[None, :], grad_scales[0], grad_values[0])

    arrived = lax.all_to_all(
        buffer.reshape(ckpts * groups, chunk, cols),
        ("ckpt", "vocab"),
        split_axis=0,
        concat_axis=0,
        tiled=True,
    ).reshape(ckpts * groups * chunk, cols)

    def part(k):
        at = lax.rem(me + k, ckpts) * quarter
        return lax.dynamic_slice(tables[0], (0, at), (rows, quarter))

    held = [part(0)]
    for k in (1, 2, 3):
        piece = part(k)
        if k == 3:
            piece, held[1] = lax.optimization_barrier((piece, held[1]))
        held.append(lax.ppermute(piece, "ckpt", [(i, (i + k) % ckpts) for i in range(ckpts)]))
    held = jnp.stack(held)

    far_me = lax.div(lax.axis_index("vocab"), near)
    near_rows = near_rows.reshape(near, far, CAP)
    passed = []
    for m in range(far):
        piece = lax.dynamic_slice(
            near_rows, (0, lax.rem(far_me + (far - m), far), 0), (near, 1, CAP)
        ).reshape(1, near * CAP)
        if m:
            piece = lax.ppermute(
                piece, "vocab", [(v, (v + groups - m * near) % groups) for v in range(groups)]
            )
        passed.append(piece)
    passed = jnp.concatenate(passed + passed, axis=0)
    arrived_rows = lax.dynamic_slice(
        passed, (lax.rem(far - far_me, far), 0), (far, near * CAP)
    ).reshape(groups * CAP, 1)
    target = arrived_rows + rows * jnp.arange(SUB, dtype=jnp.int32)
    return pl.pallas_call(
        merge_kernel,
        in_specs=[
            pl.BlockSpec(memory_space=pl.ANY),
            pl.BlockSpec(memory_space=pl.ANY),
            pl.BlockSpec(memory_space=pl.ANY),
        ],
        out_specs=pl.BlockSpec(memory_space=pltpu.HBM),
        out_shape=jax.ShapeDtypeStruct((rows, quarter), jnp.bfloat16),
        scratch_shapes=[
            pltpu.VMEM((1, groups * chunk), jnp.int32),
            pltpu.VMEM((ckpts, groups * chunk, cols), jnp.bfloat16),
            pltpu.VMEM((ckpts, rows, quarter), jnp.bfloat16),
            pltpu.VMEM((SUB * rows, groups * chunk), jnp.bfloat16),
            pltpu.VMEM((rows, quarter), jnp.float32),
            pltpu.VMEM((rows, quarter), jnp.float32),
            pltpu.VMEM((rows, quarter), jnp.bfloat16),
            pltpu.SemaphoreType.DMA((ckpts + 1,)),
            pltpu.SemaphoreType.DMA((ckpts,)),
            pltpu.SemaphoreType.DMA((SUB,)),
        ],
        compiler_params=pltpu.CompilerParams(vmem_limit_bytes=32 << 20),
        name="merge",
    )(target.reshape(1, groups * chunk), arrived, held)


def solution(mesh):
    return jax.shard_map(
        per_device,
        mesh=mesh,
        in_specs=(
            P("vocab"),
            P("ckpt", "vocab", None),
            P("ckpt", None, "vocab"),
            P("ckpt", "vocab", None),
        ),
        out_specs=P("vocab", "ckpt"),
        check_vma=False,
    )
```
